32 devices in a mesh: rep: 8 (over z, x), grp: 4 (over y, core).
Axes of the slice: x: 2, y: 2, z: 4, core: 2. Of those that a mesh axis runs over, the one named last changes fastest.
Arguments:
- tokens: bfloat16 [32768, 960], P(('rep', 'grp')), may hold values from -6 to 6
- segments: int32 [32, 1024], P(('rep', 'grp')), may hold values from 0 to 3, never falling along the last dimension, each value on 1 to 512 neighbouring positions
- norm_attn: bfloat16 [960], P('grp'), may hold values from 0.5 to 1.5
- w_query: bfloat16 [960, 960], P('grp'), may hold values from -0.1875 to 0.1875
- w_key: bfloat16 [960, 320], P('grp'), may hold values from -0.1875 to 0.1875
- w_value: bfloat16 [960, 320], P('grp'), may hold values from -0.1875 to 0.1875
- w_out: bfloat16 [960, 960], P('grp'), may hold values from -1 to 1
- norm_mlp: bfloat16 [960], P('grp'), may hold values from 0.5 to 1.5
- w_gate: bfloat16 [960, 2560], P('grp'), may hold values from -0.1875 to 0.1875
- w_up: bfloat16 [960, 2560], P('grp'), may hold values from -0.1875 to 0.1875
- w_down: bfloat16 [2560, 960], P('grp'), may hold values from -0.125 to 0.125
- cotangent: bfloat16 [32768, 960], P(('rep', 'grp')), may hold values from -6 to 6
Outputs:
- mixed: bfloat16 [32768, 960], P(('rep', 'grp'))
- grad_tokens: float32 [32768, 960], P(('rep', 'grp'))
- grad_norm_attn: float32 [960], P('grp')
- grad_w_query: float32 [960, 960], P('grp')
- grad_w_key: float32 [960, 320], P('grp')
- grad_w_value: float32 [960, 320], P('grp')
- grad_w_out: float32 [960, 960], P('grp')
- grad_norm_mlp: float32 [960], P('grp')
- grad_w_gate: float32 [960, 2560], P('grp')
- grad_w_up: float32 [960, 2560], P('grp')
- grad_w_down: float32 [2560, 960], P('grp')
The draws below stay inside these ranges and needn't reach their ends.
Inputs may be any that keep to these rules, and one draw needn't show every extreme that they name: `segments`: each row numbers the documents of one sequence in order from 0, never falling, each document 1 to 512 tokens long.
All inputs are finite; a program needn't handle non-finite values.
Results may differ from the reference program's by a relative error of at most 0.013.
Values may be sent and summed in bfloat16 or wider, within the bound.
A program may use at most 320 MiB of HBM per device.

```python
import math
import jax
import jax.numpy as jnp
import numpy as np
from jax import lax

D = 960
FF = 2560
QH = 15
KVH = 5
HD = 64
DOCS = 4
SEQ = 1024
NSEQ = 32
TOKENS = 32768


def block_scale(key, extent, shards, low, top_value):
    gain = 1.0
    for dim, shards_of in shards:
        steps = jax.random.uniform(jax.random.fold_in(jax.random.fold_in(key, 6), dim), (shards_of,), jnp.float32, low / len(shards), top_value / len(shards))
        gain = gain * jnp.repeat(jnp.exp(steps), extent[dim] // shards_of).reshape((-1,) + (1,) * (len(extent) - 1 - dim))
    return gain


def length_profile(number_of, total, most, skew):
    portions = [(1 << 20) // math.isqrt(rank ** skew) + 1 for rank in range(2, number_of + 1)]
    surplus, holding = total - most - (number_of - 1), [1] * (number_of - 1)
    while surplus > 0:
        candidates = [i for i in range(number_of - 1) if holding[i] < most]
        mass, budget = sum([portions[i] for i in candidates]), surplus
        for i in candidates:
            extra = min(most - holding[i], max(1, budget * portions[i] // mass), surplus)
            holding[i] = holding[i] + extra
            surplus = surplus - extra
    return np.array([most] + holding)


def uneven_parts(own_key, count, total, bound, skew):
    if count == 2:
        one = jax.random.randint(own_key, (), max(1, total - bound), min(bound, total - 1) + 1)
        return jnp.stack([one, total - one])
    tallies = jnp.asarray(length_profile(count, total, bound, skew), jnp.int32)
    pairs = (count - 1) // 2
    donor, receiver = tallies[1:1 + 2 * pairs:2], tallies[2:2 + 2 * pairs:2]
    slack = jnp.minimum(donor - 1, bound - receiver)
    shifted = jax.random.randint(jax.random.fold_in(own_key, 1), (pairs,), 0, 1 << 20) % (slack + 1)
    tallies = tallies.at[1:1 + 2 * pairs:2].set(donor - shifted).at[2:2 + 2 * pairs:2].set(receiver + shifted)
    return tallies[jax.random.permutation(jax.random.fold_in(own_key, 2), count)]


def normal_values(stream_key, shape, spread, reach, split=(), held_as=jnp.bfloat16):
    array = jax.random.normal(stream_key, shape, jnp.float32) * spread
    if len(split) > 0:
        array = block_scale(stream_key, shape, split, -0.22, 0.18) * array
    return jnp.clip(array, min=-reach, max=reach).astype(held_as)


def setup_inputs(seed: int = 0) -> dict:
    key_of = jax.random.split(jax.random.key(seed), 13)
    tokens = normal_values(key_of[0], (TOKENS, D), 1.0, 6.0, ((0, 32),))
    segments = jax.vmap(lambda own: jnp.searchsorted(jnp.cumsum(uneven_parts(own, DOCS, SEQ, SEQ // 2, 1)), jnp.arange(SEQ), side="right"))(jax.random.split(key_of[1], NSEQ)).reshape((NSEQ, SEQ)).astype(jnp.int32)
    norm_attn = jnp.clip(1.0 + 0.1 * jax.random.normal(key_of[2], (D,), jnp.float32), 0.5, 1.5).astype(jnp.bfloat16)
    w_query = normal_values(key_of[3], (D, QH * HD), D ** -0.5, 0.1875, ((0, 4),))
    w_key = normal_values(key_of[4], (D, KVH * HD), D ** -0.5, 0.1875, ((0, 4),))
    w_value = normal_values(key_of[5], (D, KVH * HD), D ** -0.5, 0.1875, ((0, 4),))
    w_out = normal_values(key_of[6], (QH * HD, D), (QH * HD // 32) ** -0.5, 1.0, ((0, 4),))
    norm_mlp = jnp.clip(1.0 + 0.1 * jax.random.normal(key_of[7], (D,), jnp.float32), 0.5, 1.5).astype(jnp.bfloat16)
    w_gate = normal_values(key_of[8], (D, FF), D ** -0.5, 0.1875, ((0, 4),))
    w_up = normal_values(key_of[9], (D, FF), D ** -0.5, 0.1875, ((0, 4),))
    w_down = normal_values(key_of[10], (FF, D), FF ** -0.5, 0.125, ((0, 4),))
    cotangent = normal_values(key_of[11], (TOKENS, D), 1.0, 6.0, ((0, 32),))
    return dict(tokens=tokens, segments=segments, norm_attn=norm_attn, w_query=w_query, w_key=w_key, w_value=w_value, w_out=w_out, norm_mlp=norm_mlp, w_gate=w_gate, w_up=w_up, w_down=w_down, cotangent=cotangent)


EPS = 1e-05
ROPE_BASE = 100000.0
HIGHEST = lax.Precision.HIGHEST

@jax.custom_vjp
def low(v):
    return lax.optimization_barrier(v.astype(jnp.bfloat16)).astype(jnp.float32)

@jax.custom_vjp
def low_back(v):
    return v

def low_keep(v):
    return (low(v), None)

def low_pass(kept, grad):
    return (grad,)

def back_keep(v):
    return (v, None)

def back_low(kept, grad):
    return (low(grad),)
low.defvjp(low_keep, low_pass)
low_back.defvjp(back_keep, back_low)

def positions_of(segment_row):
    length = segment_row.shape[0]
    places = jnp.arange(length, dtype=jnp.int32)
    begins = jnp.concatenate([jnp.ones((1,), dtype=jnp.bool_), segment_row[1:] != segment_row[:-1]])
    firsts = lax.cummax(jnp.where(begins, places, jnp.zeros_like(places)), axis=0)
    return places - firsts

def rope_tables(positions, head_size):
    halfway = head_size // 2
    inverse = ROPE_BASE ** (-(jnp.arange(halfway, dtype=jnp.float32) * 2.0 / head_size))
    angles = positions.astype(jnp.float32)[:, None] * inverse[None, :]
    return (jnp.cos(angles), jnp.sin(angles))

def rotate(values, cosine, sine):
    halfway = values.shape[-1] // 2
    first_half = values[..., :halfway]
    second_half = values[..., halfway:]
    cos_rows = cosine[:, None, :]
    sin_rows = sine[:, None, :]
    return jnp.concatenate([first_half * cos_rows - second_half * sin_rows, second_half * cos_rows + first_half * sin_rows], axis=-1)

def rms_scale(values):
    return lax.rsqrt(lax.optimization_barrier(jnp.mean(values * values, axis=-1, keepdims=True)) + EPS)

def matmul(left, right):
    return jnp.dot(left, right, precision=HIGHEST)

def attend(queries, keys, values, segment_row):
    length = queries.shape[0]
    block = min(512, length)
    groups = QH // KVH
    scale = HD ** (-0.5)
    blocked = queries.reshape(length // block, block, KVH, groups, HD)
    key_places = jnp.arange(length, dtype=jnp.int32)

    def one_block(item):
        query_block, offset = item
        query_places = offset + jnp.arange(block, dtype=jnp.int32)
        query_segments = lax.dynamic_slice_in_dim(segment_row, offset, block)
        scores = low_back(jnp.einsum('qkgd,tkd->kgqt', query_block, keys, precision=HIGHEST) * scale)
        allowed = (query_segments[:, None] == segment_row[None, :]) & (key_places[None, :] <= query_places[:, None])
        scores = jnp.where(allowed, scores, -1e+30)
        row_peak = lax.optimization_barrier(jnp.max(scores, axis=-1, keepdims=True))
        exponent = jnp.exp(scores - row_peak)
        probability = low(exponent / lax.optimization_barrier(jnp.sum(exponent, axis=-1, keepdims=True)))
        return jnp.einsum('kgqt,tkd->qkgd', probability, values, precision=HIGHEST)
    offsets = jnp.arange(length // block, dtype=jnp.int32) * block
    result = lax.map(jax.checkpoint(one_block), (blocked, offsets))
    return result.reshape(length, QH * HD)

def layer(inputs, gain_attn, query_w, key_w, value_w, out_w, gain_mlp, gate_w, up_w, down_w, segment_row):
    length = inputs.shape[0]
    cosine, sine = rope_tables(positions_of(segment_row), HD)
    normed_attn = low(inputs * rms_scale(inputs) * gain_attn)
    queries = low(rotate(low_back(matmul(normed_attn, query_w)).reshape(length, QH, HD), cosine, sine))
    keys = low(rotate(low_back(matmul(normed_attn, key_w)).reshape(length, KVH, HD), cosine, sine))
    values = low(low_back(matmul(normed_attn, value_w))).reshape(length, KVH, HD)
    attended = low(low_back(attend(queries, keys, values, segment_row)))
    residual = inputs + low_back(matmul(attended, out_w))
    normed_mlp = low(residual * rms_scale(residual) * gain_mlp)
    gate = low_back(matmul(normed_mlp, gate_w))
    upward = low_back(matmul(normed_mlp, up_w))
    hidden = low(jax.nn.silu(gate) * upward)
    return residual + matmul(hidden, down_w)

def reference(tokens, segments, norm_attn, w_query, w_key, w_value, w_out, norm_mlp, w_gate, w_up, w_down, cotangent):
    weights = tuple((item.astype(jnp.float32) for item in (norm_attn, w_query, w_key, w_value, w_out, norm_mlp, w_gate, w_up, w_down)))
    inputs = tokens.astype(jnp.float32).reshape(NSEQ, SEQ, D)
    upstream = cotangent.astype(jnp.float32).reshape(NSEQ, SEQ, D)

    def step(totals, item):
        sequence, segment_row, grad_out = item

        def forward(values, *params):
            return layer(values, *params, segment_row)
        output, pullback = jax.vjp(forward, sequence, *weights)
        grads = pullback(grad_out)
        new_totals = tuple((total + grad for total, grad in zip(totals, grads[1:])))
        return (new_totals, (output.astype(jnp.bfloat16), grads[0]))
    zeros = tuple((jnp.zeros(item.shape, jnp.float32) for item in weights))
    totals, (outputs, grad_inputs) = lax.scan(step, zeros, (inputs, segments, upstream))
    return (outputs.reshape(TOKENS, D), grad_inputs.reshape(TOKENS, D), totals[0], totals[1], totals[2], totals[3], totals[4], totals[5], totals[6], totals[7], totals[8])
```

```python
import jax
import jax.numpy as jnp
from jax import lax
from jax.sharding import PartitionSpec as P

QH = 15
KVH = 5
HD = 64


EPS = 1e-05
ROPE_BASE = 100000.0


def positions_of(segment_row):
    length = segment_row.shape[0]
    places = jnp.arange(length, dtype=jnp.int32)
    begins = jnp.concatenate([jnp.ones((1,), dtype=jnp.bool_), segment_row[1:] != segment_row[:-1]])
    firsts = lax.cummax(jnp.where(begins, places, jnp.zeros_like(places)), axis=0)
    return places - firsts


def rope_tables(positions, head_size):
    halfway = head_size // 2
    inverse = ROPE_BASE ** (-(jnp.arange(halfway, dtype=jnp.float32) * 2.0 / head_size))
    angles = positions.astype(jnp.float32)[:, None] * inverse[None, :]
    return (jnp.cos(angles), jnp.sin(angles))


def rotate(values, cosine, sine):
    halfway = values.shape[-1] // 2
    first_half = values[..., :halfway]
    second_half = values[..., halfway:]
    cos_rows = cosine[:, None, :]
    sin_rows = sine[:, None, :]
    return jnp.concatenate(
        [
            first_half * cos_rows - second_half * sin_rows,
            second_half * cos_rows + first_half * sin_rows,
        ],
        axis=-1,
    )


def rms_scale(values):
    return lax.rsqrt(jnp.mean(values * values, axis=-1, keepdims=True) + EPS)


def matmul(left, right):
    return jnp.dot(left, right, preferred_element_type=jnp.float32)


def left_product(rows_in, rows_grad):
    return jnp.einsum("te,tf->ef", rows_in, rows_grad, preferred_element_type=jnp.float32)


def right_product(rows_grad, weight):
    return jnp.einsum("tf,ef->te", rows_grad, weight, preferred_element_type=jnp.float32)


def norm_back(values, scale, gain, grad_normed):
    grad_gain = jnp.sum(grad_normed * values * scale, axis=0)
    scaled = grad_normed * gain.astype(jnp.float32)
    grad_values = scale * (
        scaled - values * scale * scale * jnp.mean(scaled * values, axis=-1, keepdims=True)
    )
    return (grad_gain, grad_values)


def block_scores(query_block, keys, segment_row, offset, scale):
    block = query_block.shape[0]
    length = keys.shape[0]
    query_places = offset + jnp.arange(block, dtype=jnp.int32)
    key_places = jnp.arange(length, dtype=jnp.int32)
    query_segments = segment_row[offset : offset + block]
    scores = (
        jnp.einsum("qkgd,tkd->kgqt", query_block, keys, preferred_element_type=jnp.float32) * scale
    )
    allowed = (query_segments[:, None] == segment_row[None, :]) & (
        key_places[None, :] <= query_places[:, None]
    )
    return jnp.where(allowed, scores, -1e30)


def shards(
    tokens,
    segments,
    norm_attn,
    w_query,
    w_key,
    w_value,
    w_out,
    norm_mlp,
    w_gate,
    w_up,
    w_down,
    cotangent,
):
    dim = tokens.shape[1]
    kv = w_key.shape[1]
    ff = w_gate.shape[1]
    rows = w_query.shape[0]
    pack_attn = jnp.concatenate(
        [
            w_query,
            w_key,
            w_value,
            w_out,
            jnp.pad(jnp.stack([norm_attn, norm_mlp], axis=1), ((0, 0), (0, 126))),
        ],
        axis=1,
    )
    full_attn = lax.all_gather(pack_attn, "grp", axis=0, tiled=True)
    query_full = full_attn[:, :dim]
    key_full = full_attn[:, dim : dim + kv]
    value_full = full_attn[:, dim + kv : dim + 2 * kv]
    out_full = full_attn[:, dim + 2 * kv : 2 * dim + 2 * kv]
    gain_attn = full_attn[:, 2 * dim + 2 * kv]
    gain_mlp = full_attn[:, 2 * dim + 2 * kv + 1]
    gate_full = lax.all_gather(w_gate, "grp", axis=0, tiled=True)
    up_full = lax.all_gather(w_up, "grp", axis=0, tiled=True)
    down_full = lax.all_gather(w_down, "grp", axis=0, tiled=True)
    length = tokens.shape[0]
    groups = QH // KVH
    scale = HD ** (-0.5)
    block = min(512, length)
    segment_row = segments[0]
    cosine, sine = rope_tables(positions_of(segment_row), HD)
    inputs = tokens.astype(jnp.float32)
    scale_attn = rms_scale(inputs)
    normed_attn = (inputs * scale_attn * gain_attn.astype(jnp.float32)).astype(jnp.bfloat16)
    queries = rotate(matmul(normed_attn, query_full).reshape(length, QH, HD), cosine, sine).astype(
        jnp.bfloat16
    )
    keys = rotate(matmul(normed_attn, key_full).reshape(length, KVH, HD), cosine, sine).astype(
        jnp.bfloat16
    )
    values = matmul(normed_attn, value_full).astype(jnp.bfloat16).reshape(length, KVH, HD)
    query_blocks = queries.reshape(length, KVH, groups, HD)
    outputs = []
    log_totals = []
    for offset in range(0, length, block):
        query_block = query_blocks[offset : offset + block]
        scores = block_scores(query_block, keys, segment_row, offset, scale)
        row_peak = jnp.max(scores, axis=-1, keepdims=True)
        exponent = jnp.exp(scores - row_peak)
        totals = jnp.sum(exponent, axis=-1, keepdims=True)
        probability = (exponent / totals).astype(jnp.bfloat16)
        outputs.append(
            jnp.einsum("kgqt,tkd->qkgd", probability, values, preferred_element_type=jnp.float32)
        )
        log_totals.append(row_peak + jnp.log(totals))
    attended = jnp.concatenate(outputs, axis=0).reshape(length, QH * HD).astype(jnp.bfloat16)
    residual = inputs + matmul(attended, out_full)
    scale_mlp = rms_scale(residual)
    normed_mlp = (residual * scale_mlp * gain_mlp.astype(jnp.float32)).astype(jnp.bfloat16)
    gate = matmul(normed_mlp, gate_full)
    upward = matmul(normed_mlp, up_full)
    sigmoid_gate = jax.nn.sigmoid(gate)
    silu_gate = gate * sigmoid_gate
    hidden = (silu_gate * upward).astype(jnp.bfloat16)
    mixed = (residual + matmul(hidden, down_full)).astype(jnp.bfloat16)
    grad_down = left_product(hidden, cotangent)
    grad_hidden = right_product(cotangent, down_full)
    grad_gate = (grad_hidden * upward * sigmoid_gate * (1.0 + gate * (1.0 - sigmoid_gate))).astype(
        jnp.bfloat16
    )
    grad_upward = (grad_hidden * silu_gate).astype(jnp.bfloat16)
    grad_wgate = left_product(normed_mlp, grad_gate)
    grad_wup = left_product(normed_mlp, grad_upward)
    grad_normed_mlp = right_product(grad_gate, gate_full) + right_product(grad_upward, up_full)
    grad_gain_mlp, grad_residual_norm = norm_back(residual, scale_mlp, gain_mlp, grad_normed_mlp)
    grad_residual = cotangent.astype(jnp.float32) + grad_residual_norm
    grad_gu = jnp.concatenate([grad_wgate, grad_wup], axis=1).astype(jnp.bfloat16)
    grad_down = grad_down.astype(jnp.bfloat16)
    grad_gu, grad_down, grad_residual = lax.optimization_barrier(
        (grad_gu, grad_down, grad_residual)
    )
    shard_gu = lax.psum_scatter(grad_gu, "grp", scatter_dimension=0, tiled=True)
    shard_down = lax.psum_scatter(grad_down, "grp", scatter_dimension=0, tiled=True)
    shard_gu, shard_down = lax.psum((shard_gu, shard_down), "rep")
    grad_attn = grad_residual.astype(jnp.bfloat16)
    grad_wout = left_product(attended, grad_attn)
    grad_attended = (
        right_product(grad_attn, out_full).astype(jnp.bfloat16).reshape(length, KVH, groups, HD)
    )
    grad_keys = jnp.zeros((length, KVH, HD), jnp.float32)
    grad_values = jnp.zeros((length, KVH, HD), jnp.float32)
    grad_query_blocks = []
    for index, offset in enumerate(range(0, length, block)):
        query_block = query_blocks[offset : offset + block]
        grad_block = grad_attended[offset : offset + block]
        scores = block_scores(query_block, keys, segment_row, offset, scale)
        probability = jnp.exp(scores - log_totals[index])
        prob_low = probability.astype(jnp.bfloat16)
        grad_prob = jnp.einsum(
            "qkgd,tkd->kgqt", grad_block, values, preferred_element_type=jnp.float32
        )
        inner = jnp.sum(probability * grad_prob, axis=-1, keepdims=True)
        grad_scores = (probability * (grad_prob - inner)).astype(jnp.bfloat16)
        grad_query_blocks.append(
            jnp.einsum("kgqt,tkd->qkgd", grad_scores, keys, preferred_element_type=jnp.float32)
            * scale
        )
        grad_keys = (
            grad_keys
            + jnp.einsum(
                "kgqt,qkgd->tkd", grad_scores, query_block, preferred_element_type=jnp.float32
            )
            * scale
        )
        grad_values = grad_values + jnp.einsum(
            "kgqt,qkgd->tkd", prob_low, grad_block, preferred_element_type=jnp.float32
        )
    grad_query_rot = jnp.concatenate(grad_query_blocks, axis=0).reshape(length, QH, HD)
    grad_queries = (
        rotate(grad_query_rot, cosine, -sine).reshape(length, QH * HD).astype(jnp.bfloat16)
    )
    grad_keys_low = rotate(grad_keys, cosine, -sine).reshape(length, KVH * HD).astype(jnp.bfloat16)
    grad_values_low = grad_values.reshape(length, KVH * HD).astype(jnp.bfloat16)
    grad_wquery = left_product(normed_attn, grad_queries)
    grad_wkey = left_product(normed_attn, grad_keys_low)
    grad_wvalue = left_product(normed_attn, grad_values_low)
    grad_normed_attn = (
        right_product(grad_queries, query_full)
        + right_product(grad_keys_low, key_full)
        + right_product(grad_values_low, value_full)
    )
    grad_gain_attn, grad_input_norm = norm_back(inputs, scale_attn, gain_attn, grad_normed_attn)
    grad_inputs = grad_residual + grad_input_norm
    pack_grad = jnp.concatenate(
        [
            grad_wquery,
            grad_wkey,
            grad_wvalue,
            grad_wout,
            jnp.pad(jnp.stack([grad_gain_attn, grad_gain_mlp], axis=1), ((0, 0), (0, 126))),
        ],
        axis=1,
    ).astype(jnp.bfloat16)
    shard_attn = lax.psum_scatter(pack_grad, "grp", scatter_dimension=0, tiled=True)
    shard_attn, shard_gu, shard_down = lax.optimization_barrier((shard_attn, shard_gu, shard_down))
    shard_attn = lax.psum(shard_attn, "rep").astype(jnp.float32)
    shard_query = shard_attn[:, :dim]
    shard_key = shard_attn[:, dim : dim + kv]
    shard_value = shard_attn[:, dim + kv : dim + 2 * kv]
    shard_out = shard_attn[:, dim + 2 * kv : 2 * dim + 2 * kv]
    shard_gain_attn = shard_attn[:, 2 * dim + 2 * kv]
    shard_gain_mlp = shard_attn[:, 2 * dim + 2 * kv + 1]
    shard_gate = shard_gu[:, :ff].astype(jnp.float32)
    shard_up = shard_gu[:, ff:].astype(jnp.float32)
    shard_down = shard_down.astype(jnp.float32)
    return (
        mixed,
        grad_inputs,
        shard_gain_attn,
        shard_query,
        shard_key,
        shard_value,
        shard_out,
        shard_gain_mlp,
        shard_gate,
        shard_up,
        shard_down,
    )


def solution(mesh):
    in_specs = (
        P(("rep", "grp"), None),
        P(("rep", "grp"), None),
        P("grp"),
        P("grp", None),
        P("grp", None),
        P("grp", None),
        P("grp", None),
        P("grp"),
        P("grp", None),
        P("grp", None),
        P("grp", None),
        P(("rep", "grp"), None),
    )
    out_specs = (
        P(("rep", "grp"), None),
        P(("rep", "grp"), None),
        P("grp"),
        P("grp", None),
        P("grp", None),
        P("grp", None),
        P("grp", None),
        P("grp"),
        P("grp", None),
        P("grp", None),
        P("grp", None),
    )
    return jax.shard_map(shards, mesh=mesh, in_specs=in_specs, out_specs=out_specs, check_vma=False)
```

```python
import jax
import jax.numpy as jnp
from jax import lax
from jax.experimental import pallas as pl
from jax.experimental.pallas import tpu as pltpu
from jax.sharding import PartitionSpec as P

QH = 15
KVH = 5
HD = 64
BLOCK = 256
DOC_MAX = 512


EPS = 1e-05
ROPE_BASE = 100000.0


def positions_of(segment_row):
    length = segment_row.shape[0]
    places = jnp.arange(length, dtype=jnp.int32)
    begins = jnp.concatenate([jnp.ones((1,), dtype=jnp.bool_), segment_row[1:] != segment_row[:-1]])
    firsts = lax.cummax(jnp.where(begins, places, jnp.zeros_like(places)), axis=0)
    return places - firsts


def rope_tables(positions, head_size):
    halfway = head_size // 2
    inverse = ROPE_BASE ** (-(jnp.arange(halfway, dtype=jnp.float32) * 2.0 / head_size))
    angles = positions.astype(jnp.float32)[:, None] * inverse[None, :]
    return (jnp.cos(angles), jnp.sin(angles))


def rotate(values, cosine, sine):
    halfway = values.shape[-1] // 2
    first_half = values[..., :halfway]
    second_half = values[..., halfway:]
    cos_rows = cosine[:, None, :]
    sin_rows = sine[:, None, :]
    return jnp.concatenate(
        [
            first_half * cos_rows - second_half * sin_rows,
            second_half * cos_rows + first_half * sin_rows,
        ],
        axis=-1,
    )


def rms_scale(values):
    return lax.rsqrt(jnp.mean(values * values, axis=-1, keepdims=True) + EPS)


def matmul(left, right):
    return jnp.dot(left, right, preferred_element_type=jnp.float32)


def left_product(rows_in, rows_grad):
    return jnp.einsum("te,tf->ef", rows_in, rows_grad, preferred_element_type=jnp.float32)


def right_product(rows_grad, weight):
    return jnp.einsum("tf,ef->te", rows_grad, weight, preferred_element_type=jnp.float32)


def norm_back(values, scale, gain, grad_normed):
    grad_gain = jnp.sum(grad_normed * values * scale, axis=0)
    scaled = grad_normed * gain.astype(jnp.float32)
    grad_values = scale * (
        scaled - values * scale * scale * jnp.mean(scaled * values, axis=-1, keepdims=True)
    )
    return (grad_gain, grad_values)


def dot_kernel(left, right, dims):
    return lax.dot_general(left, right, (((dims[0],), (dims[1],)), ((), ())), preferred_element_type=jnp.float32)


def allowed_block(seg_col, seg_row, low, start, stop):
    query_places = start + lax.broadcasted_iota(jnp.int32, (stop - start, stop - low), 0)
    key_places = low + lax.broadcasted_iota(jnp.int32, (stop - start, stop - low), 1)
    same = seg_col[start:stop, :] == seg_row[:, low:stop]
    return same & (key_places <= query_places)


def windows(length):
    block = min(BLOCK, length)
    for start in range(0, length, block):
        yield max(0, start - DOC_MAX), start, start + block


def attend_kernel(q_ref, k_ref, v_ref, col_ref, row_ref, o_ref, lse_ref):
    scale = HD ** (-0.5)
    for low, start, stop in windows(q_ref.shape[2]):
        allowed = allowed_block(col_ref, row_ref, low, start, stop)
        keys = k_ref[0, low:stop, :]
        values = v_ref[0, low:stop, :]
        for head in range(q_ref.shape[1]):
            scores = dot_kernel(q_ref[0, head, start:stop, :], keys, (1, 1)) * scale
            scores = jnp.where(allowed, scores, -1e30)
            peak = jnp.max(scores, axis=-1, keepdims=True)
            exponent = jnp.exp(scores - peak)
            totals = jnp.sum(exponent, axis=-1, keepdims=True)
            probability = (exponent * (1.0 / totals)).astype(jnp.bfloat16)
            o_ref[0, head, start:stop, :] = dot_kernel(probability, values, (1, 0)).astype(
                jnp.bfloat16
            )
            lse_ref[0, head, start:stop, :] = peak + jnp.log(totals)


def attend_back_kernel(
    q_ref, k_ref, v_ref, do_ref, lse_ref, col_ref, row_ref, dq_ref, dk_ref, dv_ref
):
    scale = HD ** (-0.5)
    dk_ref[...] = jnp.zeros_like(dk_ref)
    dv_ref[...] = jnp.zeros_like(dv_ref)
    for low, start, stop in windows(q_ref.shape[2]):
        allowed = allowed_block(col_ref, row_ref, low, start, stop)
        keys = k_ref[0, low:stop, :]
        values = v_ref[0, low:stop, :]
        grad_keys = jnp.zeros((stop - low, HD), jnp.float32)
        grad_values = jnp.zeros((stop - low, HD), jnp.float32)
        for head in range(q_ref.shape[1]):
            queries = q_ref[0, head, start:stop, :]
            grads = do_ref[0, head, start:stop, :]
            scores = dot_kernel(queries, keys, (1, 1)) * scale
            probability = jnp.exp(
                jnp.where(allowed, scores, -1e30) - lse_ref[0, head, start:stop, :]
            )
            grad_prob = dot_kernel(grads, values, (1, 1))
            inner = jnp.sum(probability * grad_prob, axis=-1, keepdims=True)
            grad_scores = (probability * (grad_prob - inner)).astype(jnp.bfloat16)
            dq_ref[0, head, start:stop, :] = dot_kernel(grad_scores, keys, (1, 0)) * scale
            grad_keys += dot_kernel(grad_scores, queries, (0, 0))
            grad_values += dot_kernel(probability.astype(jnp.bfloat16), grads, (0, 0))
        dk_ref[0, low:stop, :] += grad_keys * scale
        dv_ref[0, low:stop, :] += grad_values


def head_specs(length, groups):
    heads = pl.BlockSpec((1, groups, length, HD), lambda i: (i, 0, 0, 0))
    narrow = pl.BlockSpec((1, groups, length, 1), lambda i: (i, 0, 0, 0))
    shared = pl.BlockSpec((1, length, HD), lambda i: (i, 0, 0))
    column = pl.BlockSpec((length, 1), lambda i: (0, 0))
    row = pl.BlockSpec((1, length), lambda i: (0, 0))
    return heads, narrow, shared, column, row


def attend(q, k, v, segments):
    kvh, groups, length, _ = q.shape
    heads, narrow, shared, column, row = head_specs(length, groups)
    return pl.pallas_call(
        attend_kernel,
        grid=(kvh,),
        out_shape=(
            jax.ShapeDtypeStruct(q.shape, jnp.bfloat16),
            jax.ShapeDtypeStruct((kvh, groups, length, 1), jnp.float32),
        ),
        in_specs=[heads, shared, shared, column, row],
        out_specs=(heads, narrow),
        compiler_params=pltpu.CompilerParams(vmem_limit_bytes=40 * 1024 * 1024),
        cost_estimate=pl.CostEstimate(
            flops=20_000_000_000, bytes_accessed=20_000_000, transcendentals=8_000_000
        ),
        name="attend",
    )(q, k, v, segments.reshape(length, 1), segments)


def attend_back(q, k, v, grads, lse, segments):
    kvh, groups, length, _ = q.shape
    heads, narrow, shared, column, row = head_specs(length, groups)
    return pl.pallas_call(
        attend_back_kernel,
        grid=(kvh,),
        out_shape=(
            jax.ShapeDtypeStruct(q.shape, jnp.float32),
            jax.ShapeDtypeStruct(k.shape, jnp.float32),
            jax.ShapeDtypeStruct(k.shape, jnp.float32),
        ),
        in_specs=[heads, shared, shared, heads, narrow, column, row],
        out_specs=(heads, shared, shared),
        compiler_params=pltpu.CompilerParams(vmem_limit_bytes=48 * 1024 * 1024),
        cost_estimate=pl.CostEstimate(
            flops=50_000_000_000, bytes_accessed=30_000_000, transcendentals=8_000_000
        ),
        name="attend_back",
    )(q, k, v, grads, lse, segments.reshape(length, 1), segments)


def shards(
    tokens,
    segments,
    norm_attn,
    w_query,
    w_key,
    w_value,
    w_out,
    norm_mlp,
    w_gate,
    w_up,
    w_down,
    cotangent,
):
    dim = tokens.shape[1]
    kv = w_key.shape[1]
    ff = w_gate.shape[1]
    rows = w_query.shape[0]
    pack_attn = jnp.concatenate(
        [
            w_query,
            w_key,
            w_value,
            w_out,
            jnp.pad(jnp.stack([norm_attn, norm_mlp], axis=1), ((0, 0), (0, 126))),
        ],
        axis=1,
    )
    full_attn = lax.all_gather(pack_attn, "grp", axis=0, tiled=True)
    query_full = full_attn[:, :dim]
    key_full = full_attn[:, dim : dim + kv]
    value_full = full_attn[:, dim + kv : dim + 2 * kv]
    out_full = full_attn[:, dim + 2 * kv : 2 * dim + 2 * kv]
    gain_attn = full_attn[:, 2 * dim + 2 * kv]
    gain_mlp = full_attn[:, 2 * dim + 2 * kv + 1]
    gate_full = lax.all_gather(w_gate, "grp", axis=0, tiled=True)
    up_full = lax.all_gather(w_up, "grp", axis=0, tiled=True)
    down_full = lax.all_gather(w_down, "grp", axis=0, tiled=True)
    length = tokens.shape[0]
    groups = QH // KVH
    segment_row = segments[0]
    cosine, sine = rope_tables(positions_of(segment_row), HD)
    inputs = tokens.astype(jnp.float32)
    scale_attn = rms_scale(inputs)
    normed_attn = (inputs * scale_attn * gain_attn.astype(jnp.float32)).astype(jnp.bfloat16)
    queries = rotate(matmul(normed_attn, query_full).reshape(length, QH, HD), cosine, sine).astype(
        jnp.bfloat16
    )
    keys = rotate(matmul(normed_attn, key_full).reshape(length, KVH, HD), cosine, sine).astype(
        jnp.bfloat16
    )
    values = matmul(normed_attn, value_full).astype(jnp.bfloat16).reshape(length, KVH, HD)
    query_heads = queries.reshape(length, KVH, groups, HD).transpose(1, 2, 0, 3)
    key_heads = keys.transpose(1, 0, 2)
    value_heads = values.transpose(1, 0, 2)
    attended, log_totals = attend(query_heads, key_heads, value_heads, segments)
    attended = attended.transpose(2, 0, 1, 3).reshape(length, QH * HD)
    residual = inputs + matmul(attended, out_full)
    scale_mlp = rms_scale(residual)
    normed_mlp = (residual * scale_mlp * gain_mlp.astype(jnp.float32)).astype(jnp.bfloat16)
    gate = matmul(normed_mlp, gate_full)
    upward = matmul(normed_mlp, up_full)
    sigmoid_gate = jax.nn.sigmoid(gate)
    silu_gate = gate * sigmoid_gate
    hidden = (silu_gate * upward).astype(jnp.bfloat16)
    mixed = (residual + matmul(hidden, down_full)).astype(jnp.bfloat16)
    grad_down = left_product(hidden, cotangent)
    grad_hidden = right_product(cotangent, down_full)
    grad_gate = (grad_hidden * upward * sigmoid_gate * (1.0 + gate * (1.0 - sigmoid_gate))).astype(
        jnp.bfloat16
    )
    grad_upward = (grad_hidden * silu_gate).astype(jnp.bfloat16)
    grad_wgate = left_product(normed_mlp, grad_gate)
    grad_wup = left_product(normed_mlp, grad_upward)
    grad_normed_mlp = right_product(grad_gate, gate_full) + right_product(grad_upward, up_full)
    grad_gain_mlp, grad_residual_norm = norm_back(residual, scale_mlp, gain_mlp, grad_normed_mlp)
    grad_residual = cotangent.astype(jnp.float32) + grad_residual_norm
    grad_gu = jnp.concatenate([grad_wgate, grad_wup], axis=1).astype(jnp.bfloat16)
    grad_down = grad_down.astype(jnp.bfloat16)
    grad_gu, grad_down, grad_residual = lax.optimization_barrier(
        (grad_gu, grad_down, grad_residual)
    )
    shard_gu = lax.psum_scatter(grad_gu, "grp", scatter_dimension=0, tiled=True)
    shard_down = lax.psum_scatter(grad_down, "grp", scatter_dimension=0, tiled=True)
    shard_gu, shard_down = lax.psum((shard_gu, shard_down), "rep")
    grad_attn = grad_residual.astype(jnp.bfloat16)
    grad_wout = left_product(attended, grad_attn)
    grad_attended = (
        right_product(grad_attn, out_full)
        .astype(jnp.bfloat16)
        .reshape(length, KVH, groups, HD)
        .transpose(1, 2, 0, 3)
    )
    grad_query_rot, grad_keys, grad_values = attend_back(
        query_heads, key_heads, value_heads, grad_attended, log_totals, segments
    )
    grad_query_rot = grad_query_rot.transpose(2, 0, 1, 3).reshape(length, QH, HD)
    grad_keys = grad_keys.transpose(1, 0, 2)
    grad_values = grad_values.transpose(1, 0, 2)
    grad_queries = (
        rotate(grad_query_rot, cosine, -sine).reshape(length, QH * HD).astype(jnp.bfloat16)
    )
    grad_keys_low = rotate(grad_keys, cosine, -sine).reshape(length, KVH * HD).astype(jnp.bfloat16)
    grad_values_low = grad_values.reshape(length, KVH * HD).astype(jnp.bfloat16)
    grad_wquery = left_product(normed_attn, grad_queries)
    grad_wkey = left_product(normed_attn, grad_keys_low)
    grad_wvalue = left_product(normed_attn, grad_values_low)
    grad_normed_attn = (
        right_product(grad_queries, query_full)
        + right_product(grad_keys_low, key_full)
        + right_product(grad_values_low, value_full)
    )
    grad_gain_attn, grad_input_norm = norm_back(inputs, scale_attn, gain_attn, grad_normed_attn)
    grad_inputs = grad_residual + grad_input_norm
    pack_grad = jnp.concatenate(
        [
            grad_wquery,
            grad_wkey,
            grad_wvalue,
            grad_wout,
            jnp.pad(jnp.stack([grad_gain_attn, grad_gain_mlp], axis=1), ((0, 0), (0, 126))),
        ],
        axis=1,
    ).astype(jnp.bfloat16)
    shard_attn = lax.psum_scatter(pack_grad, "grp", scatter_dimension=0, tiled=True)
    shard_attn, shard_gu, shard_down = lax.optimization_barrier((shard_attn, shard_gu, shard_down))
    shard_attn = lax.psum(shard_attn, "rep").astype(jnp.float32)
    shard_query = shard_attn[:, :dim]
    shard_key = shard_attn[:, dim : dim + kv]
    shard_value = shard_attn[:, dim + kv : dim + 2 * kv]
    shard_out = shard_attn[:, dim + 2 * kv : 2 * dim + 2 * kv]
    shard_gain_attn = shard_attn[:, 2 * dim + 2 * kv]
    shard_gain_mlp = shard_attn[:, 2 * dim + 2 * kv + 1]
    shard_gate = shard_gu[:, :ff].astype(jnp.float32)
    shard_up = shard_gu[:, ff:].astype(jnp.float32)
    shard_down = shard_down.astype(jnp.float32)
    return (
        mixed,
        grad_inputs,
        shard_gain_attn,
        shard_query,
        shard_key,
        shard_value,
        shard_out,
        shard_gain_mlp,
        shard_gate,
        shard_up,
        shard_down,
    )


def solution(mesh):
    in_specs = (
        P(("rep", "grp"), None),
        P(("rep", "grp"), None),
        P("grp"),
        P("grp", None),
        P("grp", None),
        P("grp", None),
        P("grp", None),
        P("grp"),
        P("grp", None),
        P("grp", None),
        P("grp", None),
        P(("rep", "grp"), None),
    )
    out_specs = (
        P(("rep", "grp"), None),
        P(("rep", "grp"), None),
        P("grp"),
        P("grp", None),
        P("grp", None),
        P("grp", None),
        P("grp", None),
        P("grp"),
        P("grp", None),
        P("grp", None),
        P("grp", None),
    )
    return jax.shard_map(shards, mesh=mesh, in_specs=in_specs, out_specs=out_specs, check_vma=False)
```
